32 devices in a mesh: dp: 32 (over z, y, x, core).
Axes of the slice: x: 2, y: 2, z: 4, core: 2. Of those that a mesh axis runs over, the one named last changes fastest.
Arguments:
- image_embed: float32 [16384, 1152], P('dp'), may hold values from -0.72 to 0.72
- text_embed: float32 [16384, 1152], P('dp'), may hold values from -0.72 to 0.72
- positives: int32 [16384], P('dp'), may hold values from 0 to 16383, as said below
Outputs:
- loss_rows: float32 [16384], P('dp')
- grad_image: float32 [16384, 1152], P('dp')
- grad_text: float32 [16384, 1152], P('dp')
The draws below stay inside these ranges and needn't reach their ends.
Inputs may be any that keep to these rules, and one draw needn't show every extreme that they name: `positives`: the positive of image row i is text row ((b - k) mod (32)) * 512 + i mod 512, with b = i // 512 and k per row in 0 .. 3.
All inputs are finite; a program needn't handle non-finite values.
Results may differ from the reference program's by a relative error of at most 0.00015.
Values sent between devices are 32-bit elements; how exact they have to be, the bound alone decides.
A program may use at most 64 MiB of HBM per device.

```python
import jax
import jax.numpy as jnp
from jax import lax

D = 1152
TOK_DEV = 512
STEPS = 3
TOKENS = 16384


def draw_positives(key, part):
    key = jax.random.fold_in(key, 5)
    blocks = TOKENS // TOK_DEV
    places = jnp.arange(TOKENS, dtype=jnp.int32)
    offsets = jax.random.randint(key, (TOKENS,), 0, STEPS + 1, dtype=jnp.int32)
    offsets = offsets.at[0].set(0).at[TOKENS - 1].set(0)
    owner = (places // TOK_DEV - offsets + blocks) % blocks
    return (owner * TOK_DEV + places % TOK_DEV).astype(jnp.int32)


def steps_of(key, extent, shards, smallest, high):
    def one(dim, blocks):
        heights = jax.random.uniform(jax.random.fold_in(jax.random.fold_in(key, 6), dim), (blocks,), jnp.float32, smallest / len(shards), high / len(shards))
        return jnp.repeat(jnp.exp(heights), extent[dim] // blocks).reshape((-1,) + (1,) * (len(extent) - dim - 1))

    level = one(*shards[0])
    for cut in shards[1:]:
        level = level * one(*cut)
    return level


def gaussian(key, dims, width, reach, shards=(), kind=jnp.bfloat16):
    result = width * jax.random.normal(key, dims, jnp.float32)
    if shards:
        result = result * steps_of(key, dims, shards, -0.22, 0.18)
    return jnp.clip(result, -reach, reach).astype(kind)


def setup_inputs(seed: int = 0) -> dict:
    splits = jax.random.split(jax.random.key(seed), 4)
    return {
        "image_embed": gaussian(splits[0], (TOKENS, D), 0.12, 0.72, ((0, 32),), jnp.float32),
        "text_embed": gaussian(splits[1], (TOKENS, D), 0.12, 0.72, ((0, 32),), jnp.float32),
        "positives": draw_positives(jax.random.fold_in(splits[3], 71), 0),
    }


def reference(image_embed, text_embed, positives):
    blocks = TOKENS // TOK_DEV
    images = image_embed.reshape(blocks, TOK_DEV, D)
    texts = text_embed.reshape(blocks, TOK_DEV, D)
    wanted = positives.reshape(blocks, TOK_DEV)
    loss_rows = jnp.zeros((blocks, TOK_DEV), jnp.float32)
    grad_image = jnp.zeros((blocks, TOK_DEV, D), jnp.float32)
    grad_text = jnp.zeros((blocks, TOK_DEV, D), jnp.float32)
    for step in range(STEPS + 1):
        window = jnp.roll(texts, step, axis=0)
        owner = (jnp.arange(blocks, dtype=jnp.int32) - step) % blocks
        columns = owner[:, None] * TOK_DEV + jnp.arange(TOK_DEV, dtype=jnp.int32)[None, :]
        scores = jnp.einsum("bid,bjd->bij", images, window, precision=lax.Precision.HIGHEST)
        logits = 10.0 * scores - 10.0
        match = wanted[:, :, None] == columns[:, None, :]
        signs = jnp.where(match, 1.0, -1.0).astype(jnp.float32)
        loss_rows = loss_rows + jnp.sum(jax.nn.softplus(-signs * logits), axis=2) / TOK_DEV
        weight = (jax.nn.sigmoid(logits) - match.astype(jnp.float32)) / TOK_DEV
        grad_image = grad_image + 10.0 * jnp.einsum("bij,bjd->bid", weight, window, precision=lax.Precision.HIGHEST)
        part = 10.0 * jnp.einsum("bij,bid->bjd", weight, images, precision=lax.Precision.HIGHEST)
        grad_text = grad_text + jnp.roll(part, -step, axis=0)
    return loss_rows.reshape(TOKENS), grad_image.reshape(TOKENS, D), grad_text.reshape(TOKENS, D)
```

```python
import functools

import jax
import jax.numpy as jnp
from jax import lax
from jax.experimental import pallas as pl
from jax.experimental.pallas import tpu as pltpu
from jax.sharding import PartitionSpec as P

MESH = pl.DeviceIdType.MESH
F32 = jnp.float32
BF16 = jnp.bfloat16
CHUNK = 256


def split(x):
    high = x.astype(BF16)
    return high, (x - high.astype(F32)).astype(BF16)


def dot(a, b, contract):
    return lax.dot_general(a, b, (((1,), (contract,)), ((), ())), preferred_element_type=F32)


def kernel(n, image, text, positives, grad_image, grad_text, loss, buf, high, low, total, places,
           send_sem, recv_sem, place_send, place_recv):
    rows = image.shape[0]
    chunk = min(CHUNK, rows)
    chunks = rows // chunk
    me = lax.axis_index("dp")
    odd = lax.rem(me, 2)
    partner = me + 1 - 2 * odd

    def at(offset):
        return lax.rem(me + offset + n, n)

    def piece(c):
        return pl.ds(pl.multiple_of(c * chunk, chunk), chunk)

    def remote(src, side, slot, c, lane, device):
        return pltpu.make_async_remote_copy(
            src_ref=src, dst_ref=buf.at[side, slot, piece(c)],
            send_sem=send_sem.at[lane, c], recv_sem=recv_sem.at[side, slot, c],
            device_id=(device,), device_id_type=MESH)

    def far_copies(c):
        return (
            remote(text.at[piece(c)], 0, 2, c, 0, at(2)),
            remote(image.at[piece(c)], 1, 2, c, 1, at(-2)),
        )

    def near_copies(c):
        return (
            remote(text.at[piece(c)], 0, 2 * odd + 1, c, 2, at(1 + 2 * odd)),
            remote(image.at[piece(c)], 1, 3 - 2 * odd, c, 3, at(2 * odd - 3)),
        )

    def forwards(c):
        return (
            remote(buf.at[0, 2, piece(c)], 0, 3 - 2 * odd, c, 4, partner),
            remote(buf.at[1, 2, piece(c)], 1, 2 * odd + 1, c, 5, partner),
        )

    def local(side, c):
        src = (text, image)[side]
        return pltpu.make_async_copy(src.at[piece(c)], buf.at[side, 0, piece(c)], recv_sem.at[side, 0, c])

    def place_copy(k):
        return pltpu.make_async_remote_copy(
            src_ref=places.at[0], dst_ref=places.at[k], send_sem=place_send.at[k],
            recv_sem=place_recv.at[k], device_id=(at(-k),), device_id_type=MESH)

    def arrived(side, k, c):
        ref = buf.at[side, k, piece(c)]
        pltpu.make_async_copy(ref, ref, recv_sem.at[side, k, c]).wait()

    for c in range(chunks):
        for side in range(2):
            local(side, c).start()
    places[0] = positives[...]

    barrier = pltpu.get_barrier_semaphore()
    for offset in (-3, -2, -1, 1, 2, 3):
        pl.semaphore_signal(barrier, inc=1, device_id=(at(offset),), device_id_type=MESH)
    pl.semaphore_wait(barrier, 6)

    for c in range(chunks):
        for copy in far_copies(c):
            copy.start()
    for c in range(chunks):
        for copy in near_copies(c):
            copy.start()
    for k in range(1, 4):
        place_copy(k).start()

    for c in range(chunks):
        for side in range(2):
            local(side, c).wait()
    for side in range(2):
        high[side], low[side] = split(buf[1 - side, 0])
    for k in range(1, 4):
        place_copy(k).wait_recv()

    grad_image[...] = jnp.zeros_like(grad_image)
    grad_text[...] = jnp.zeros_like(grad_text)
    total[...] = jnp.zeros_like(total)

    def unit(side, k, c):
        out = (grad_image, grad_text)[side]
        b_high, b_low = split(buf[side, k, piece(c), :])
        scores = (dot(high[side], b_high, 1) + dot(high[side], b_low, 1)) + dot(low[side], b_high, 1)
        logits = 10.0 * scores - 10.0
        wanted = places[0 if side == 0 else k, 0:1, piece(c)]
        block = lax.rem(me - k + n, n) if side == 0 else me
        lanes = lax.broadcasted_iota(jnp.int32, (1, chunk), 1) + c * chunk
        column = jnp.where(wanted == block * rows + lanes, lanes, -1)
        match = lax.broadcasted_iota(jnp.int32, (rows, chunk), 0) == column
        decay = jnp.exp(-jnp.abs(logits))
        inverse = 1.0 / (1.0 + decay)
        sigmoid = jnp.where(logits >= 0.0, inverse, decay * inverse)
        weight = (sigmoid - match.astype(F32)) * (10.0 / rows)
        if side == 0:
            signed = jnp.where(match, -logits, logits)
            part = jnp.maximum(signed, 0.0) + jnp.log1p(decay)
            for s in range(0, chunk, 128):
                total[...] += part[:, s:s + 128]
        w_high, w_low = split(weight)
        out[...] += (dot(w_high, b_high, 0) + dot(w_low, b_high, 0)) + dot(w_high, b_low, 0)

    def step(s, carry):
        c = s // 4
        r = lax.rem(s, 4)
        k_text = lax.rem(r * (3 - 2 * odd), 4)
        k_image = lax.rem(r * (1 + 2 * odd), 4)

        @pl.when(r > 0)
        def _():
            arrived(0, k_text, c)
            arrived(1, k_image, c)

        @pl.when(r == 2)
        def _():
            for copy in forwards(c):
                copy.start()

        unit(0, k_text, c)
        unit(1, k_image, c)
        return carry

    lax.fori_loop(0, 4 * chunks, step, 0)
    loss[...] = jnp.sum(total[...].T, axis=0, keepdims=True) * (1.0 / rows)

    for c in range(chunks):
        for copy in far_copies(c) + near_copies(c) + forwards(c):
            copy.wait_send()
    for k in range(1, 4):
        place_copy(k).wait_send()


def per_device(n, image_embed, text_embed, positives):
    rows, width = image_embed.shape
    chunks = rows // min(CHUNK, rows)
    vmem = pl.BlockSpec(memory_space=pltpu.VMEM)
    anywhere = pl.BlockSpec(memory_space=pl.ANY)
    block = jax.ShapeDtypeStruct((rows, width), F32)
    grad_image, grad_text, loss = pl.pallas_call(
        functools.partial(kernel, n),
        out_shape=(block, block, jax.ShapeDtypeStruct((1, rows), F32)),
        in_specs=[anywhere, anywhere, vmem],
        out_specs=(vmem, vmem, vmem),
        scratch_shapes=[
            pltpu.VMEM((2, 4, rows, width), F32),
            pltpu.VMEM((2, rows, width), BF16),
            pltpu.VMEM((2, rows, width), BF16),
            pltpu.VMEM((rows, 128), F32),
            pltpu.VMEM((4, 8, rows), jnp.int32),
            pltpu.SemaphoreType.DMA((6, chunks)),
            pltpu.SemaphoreType.DMA((2, 4, chunks)),
            pltpu.SemaphoreType.DMA((4,)),
            pltpu.SemaphoreType.DMA((4,)),
        ],
        compiler_params=pltpu.CompilerParams(
            collective_id=0, has_side_effects=True, vmem_limit_bytes=60 * 2**20),
        cost_estimate=pl.CostEstimate(
            flops=2 * 16 * 3 * rows * rows * width, bytes_accessed=16 * rows * width,
            transcendentals=8 * rows * rows),
    )(image_embed, text_embed, jnp.broadcast_to(positives[None, :], (8, rows)))
    return loss.reshape(rows), grad_image, grad_text


def solution(mesh):
    placed = (P("dp", None), P("dp", None), P("dp"))
    return jax.shard_map(
        functools.partial(per_device, mesh.shape["dp"]),
        mesh=mesh,
        in_specs=placed,
        out_specs=(P("dp"), P("dp", None), P("dp", None)),
        check_vma=False,
    )
```

```python
import functools

import jax
import jax.numpy as jnp
from jax import lax
from jax.experimental import pallas as pl
from jax.experimental.pallas import tpu as pltpu
from jax.sharding import PartitionSpec as P

MESH = pl.DeviceIdType.MESH
F32 = jnp.float32
BF16 = jnp.bfloat16
CHUNK = 128


def split(x):
    high = x.astype(BF16)
    return high, (x - high.astype(F32)).astype(BF16)


def dot(a, b, contract):
    return lax.dot_general(a, b, (((1,), (contract,)), ((), ())), preferred_element_type=F32)


def kernel(n, chunk, image, text, positives, grad_image, grad_text, loss, buf, three, total, places,
           send_sem, recv_sem, place_send, place_recv):
    rows = image.shape[0]
    chunks = rows // chunk
    me = lax.axis_index("dp")
    odd = lax.rem(me, 2)
    place = lax.rem(me, 4)
    partner = me + 1 - 2 * odd

    def at(offset):
        return lax.rem(me + offset + n, n)

    def piece(c):
        return pl.ds(pl.multiple_of(c * chunk, chunk), chunk)

    def remote(src, side, slot, c, lane, device):
        return pltpu.make_async_remote_copy(
            src_ref=src, dst_ref=buf.at[side, slot, piece(c)],
            send_sem=send_sem.at[lane, c], recv_sem=recv_sem.at[side, slot, c],
            device_id=(device,), device_id_type=MESH)

    def far_text(c):
        return remote(text.at[piece(c)], 0, 2, c, 0, at(2))

    def far_image(c):
        return remote(image.at[piece(c)], 1, 2, c, 1, at(-2))

    def relay_text(c):
        return remote(buf.at[0, 3, piece(c)], 0, 2, c, 6, at(-1))

    def relay_image(c):
        return remote(buf.at[1, 3, piece(c)], 1, 2, c, 6, at(1))

    def near_text(c):
        return remote(text.at[piece(c)], 0, 2 * odd + 1, c, 2, at(1 + 2 * odd))

    def near_image(c):
        return remote(image.at[piece(c)], 1, 3 - 2 * odd, c, 3, at(2 * odd - 3))

    def pass_text(c):
        return remote(buf.at[0, 2, piece(c)], 0, 3 - 2 * odd, c, 4, partner)

    def pass_image(c):
        return remote(buf.at[1, 2, piece(c)], 1, 2 * odd + 1, c, 5, partner)

    def local(side, c):
        src = (text, image)[side]
        return pltpu.make_async_copy(src.at[piece(c)], buf.at[side, 0, piece(c)], recv_sem.at[side, 0, c])

    def place_copy(k):
        return pltpu.make_async_remote_copy(
            src_ref=places.at[0], dst_ref=places.at[k], send_sem=place_send.at[k],
            recv_sem=place_recv.at[k], device_id=(at(-k),), device_id_type=MESH)

    def arrived(side, k, c):
        ref = buf.at[side, k, piece(c)]
        pltpu.make_async_copy(ref, ref, recv_sem.at[side, k, c]).wait()

    for c in range(chunks):
        for side in range(2):
            local(side, c).start()
    places[0] = jnp.broadcast_to(positives[...], places.shape[1:])

    barrier = pltpu.get_barrier_semaphore()
    for offset in (-3, -2, -1, 1, 2, 3):
        pl.semaphore_signal(barrier, inc=1, device_id=(at(offset),), device_id_type=MESH)
    pl.semaphore_wait(barrier, 6)

    for c in range(chunks):
        near_text(c).start()
        near_image(c).start()

        @pl.when(place != 3)
        def _():
            far_text(c).start()

        @pl.when(place != 0)
        def _():
            far_image(c).start()
    for k in range(1, 4):
        place_copy(k).start()

    for c in range(chunks):
        for side in range(2):
            local(side, c).wait()
    for side in range(2):
        a_high, a_low = split(buf[1 - side, 0])
        three[side] = jnp.concatenate([a_high, a_high, a_low], axis=1)

    def unit(side, parts, first=False):
        out = (grad_image, grad_text)[side]
        b_high, b_low = split(jnp.concatenate([buf[side, k, pl.ds(row, size), :] for k, row, size in parts], axis=0))
        scores = dot(three[side], jnp.concatenate([b_high, b_low, b_high], axis=1), 1)
        logits = 10.0 * scores - 10.0
        columns = []
        for k, row, size in parts:
            wanted = places[0 if side == 0 else k, 0:1, pl.ds(row, size)]
            block = lax.rem(me - k + n, n) if side == 0 else me
            lanes = lax.broadcasted_iota(jnp.int32, (1, size), 1) + row
            columns.append(jnp.where(wanted == block * rows + lanes, lanes, -1))
        column = jnp.concatenate(columns, axis=1)
        match = lax.broadcasted_iota(jnp.int32, scores.shape, 0) == column
        decay = jnp.exp(-jnp.abs(logits))
        inverse = 1.0 / (1.0 + decay)
        sigmoid = jnp.where(logits >= 0.0, inverse, decay * inverse)
        weight = (sigmoid - match.astype(F32)) * (10.0 / rows)
        w_high, w_low = split(weight)
        grad = dot(jnp.concatenate([w_high, w_low, w_high], axis=1),
                   jnp.concatenate([b_high, b_high, b_low], axis=0), 0)
        if first:
            out[...] = grad
        else:
            out[...] += grad
        if side == 0:
            signed = jnp.where(match, -logits, logits)
            part = jnp.maximum(signed, 0.0) + jnp.log1p(decay)
            folded = part[:, :128]
            for s in range(128, part.shape[1], 128):
                folded += part[:, s:s + 128]
            if first:
                total[...] = folded
            else:
                total[...] += folded

    for side in range(2):
        unit(side, [(0, 0, rows)], first=True)
    for k in range(1, 4):
        place_copy(k).wait_recv()

    early_text, early_image = 3 - 2 * odd, 1 + 2 * odd
    late_text, late_image = 1 + 2 * odd, 3 - 2 * odd

    def near_step(c):
        arrived(0, early_text, c)
        arrived(1, early_image, c)

        @pl.when(place == 2)
        def _():
            relay_text(c).start()

        @pl.when(place == 1)
        def _():
            relay_image(c).start()

    def step(c, carry):
        arrived(0, 2, c)
        pass_text(c).start()
        arrived(1, 2, c)
        pass_image(c).start()

        @pl.when(c + 1 < chunks)
        def _():
            near_step(c + 1)

        row = pl.multiple_of(c * chunk, chunk)
        arrived(0, late_text, c)
        unit(0, [(2, row, chunk), (late_text, row, chunk)])
        arrived(1, late_image, c)
        unit(1, [(2, row, chunk), (late_image, row, chunk)])

        @pl.when(c == chunks - 2)
        def _():
            unit(0, [(early_text, 0, rows)])
            unit(1, [(early_image, 0, rows)])

        return carry

    near_step(0)
    lax.fori_loop(0, chunks, step, 0)
    loss[...] = jnp.sum(total[...].T, axis=0, keepdims=True) * (1.0 / rows)

    for c in range(chunks):
        near_text(c).wait_send()
        near_image(c).wait_send()
        pass_text(c).wait_send()
        pass_image(c).wait_send()

        @pl.when(place != 3)
        def _():
            far_text(c).wait_send()

        @pl.when(place != 0)
        def _():
            far_image(c).wait_send()

        @pl.when(place == 2)
        def _():
            relay_text(c).wait_send()

        @pl.when(place == 1)
        def _():
            relay_image(c).wait_send()
    for k in range(1, 4):
        place_copy(k).wait_send()


def per_device(n, image_embed, text_embed, positives):
    rows, width = image_embed.shape
    chunk = CHUNK if rows % CHUNK == 0 and rows > CHUNK else rows // 2
    chunks = rows // chunk
    vmem = pl.BlockSpec(memory_space=pltpu.VMEM)
    anywhere = pl.BlockSpec(memory_space=pl.ANY)
    block = jax.ShapeDtypeStruct((rows, width), F32)
    grad_image, grad_text, loss = pl.pallas_call(
        functools.partial(kernel, n, chunk),
        out_shape=(block, block, jax.ShapeDtypeStruct((1, rows), F32)),
        in_specs=[anywhere, anywhere, vmem],
        out_specs=(vmem, vmem, vmem),
        scratch_shapes=[
            pltpu.VMEM((2, 4, rows, width), F32),
            pltpu.VMEM((2, rows, 3 * width), BF16),
            pltpu.VMEM((rows, 128), F32),
            pltpu.VMEM((4, 8, rows), jnp.int32),
            pltpu.SemaphoreType.DMA((7, chunks)),
            pltpu.SemaphoreType.DMA((2, 4, chunks)),
            pltpu.SemaphoreType.DMA((4,)),
            pltpu.SemaphoreType.DMA((4,)),
        ],
        compiler_params=pltpu.CompilerParams(
            collective_id=0, has_side_effects=True, vmem_limit_bytes=60 * 2**20),
        cost_estimate=pl.CostEstimate(
            flops=2 * 16 * 3 * rows * rows * width, bytes_accessed=16 * rows * width,
            transcendentals=8 * rows * rows),
    )(image_embed, text_embed, positives.reshape(1, rows))
    return loss.reshape(rows), grad_image, grad_text


def solution(mesh):
    placed = (P("dp", None), P("dp", None), P("dp"))
    return jax.shard_map(
        functools.partial(per_device, mesh.shape["dp"]),
        mesh=mesh,
        in_specs=placed,
        out_specs=(P("dp"), P("dp", None), P("dp", None)),
        check_vma=False,
    )
```

```python
import functools

import jax
import jax.numpy as jnp
from jax import lax
from jax.experimental import pallas as pl
from jax.experimental.pallas import tpu as pltpu
from jax.sharding import PartitionSpec as P

MESH = pl.DeviceIdType.MESH
F32 = jnp.float32
BF16 = jnp.bfloat16
CHUNK = 128


def split(x):
    high = x.astype(BF16)
    return high, (x - high.astype(F32)).astype(BF16)


def dot(a, b, contract):
    return lax.dot_general(a, b, (((1,), (contract,)), ((), ())), preferred_element_type=F32)


def kernel(n, chunk, image, text, positives, grad_image, grad_text, loss, buf, three, total, places,
           send_sem, recv_sem, place_send, place_recv):
    rows = image.shape[0]
    chunks = rows // chunk
    me = lax.axis_index("dp")
    odd = lax.rem(me, 2)
    place = lax.rem(me, 4)
    partner = me + 1 - 2 * odd

    def at(offset):
        return lax.rem(me + offset + n, n)

    def piece(c):
        return pl.ds(pl.multiple_of(c * chunk, chunk), chunk)

    def remote(src, side, slot, c, lane, device):
        return pltpu.make_async_remote_copy(
            src_ref=src, dst_ref=buf.at[side, slot, piece(c)],
            send_sem=send_sem.at[lane, c], recv_sem=recv_sem.at[side, slot, c],
            device_id=(device,), device_id_type=MESH)

    def far_text(c):
        return remote(text.at[piece(c)], 0, 2, c, 0, at(2))

    def far_image(c):
        return remote(image.at[piece(c)], 1, 2, c, 1, at(-2))

    def relay_text(c):
        return remote(buf.at[0, 3, piece(c)], 0, 2, c, 6, at(-1))

    def relay_image(c):
        return remote(buf.at[1, 3, piece(c)], 1, 2, c, 6, at(1))

    def near_text(c):
        return remote(text.at[piece(c)], 0, 2 * odd + 1, c, 2, at(1 + 2 * odd))

    def near_image(c):
        return remote(image.at[piece(c)], 1, 3 - 2 * odd, c, 3, at(2 * odd - 3))

    def pass_text(c):
        return remote(buf.at[0, 2, piece(c)], 0, 3 - 2 * odd, c, 4, partner)

    def pass_image(c):
        return remote(buf.at[1, 2, piece(c)], 1, 2 * odd + 1, c, 5, partner)

    def local(side, c):
        src = (text, image)[side]
        return pltpu.make_async_copy(src.at[piece(c)], buf.at[side, 0, piece(c)], recv_sem.at[side, 0, c])

    def place_copy(k):
        return pltpu.make_async_remote_copy(
            src_ref=places.at[0], dst_ref=places.at[k], send_sem=place_send.at[k],
            recv_sem=place_recv.at[k], device_id=(at(-k),), device_id_type=MESH)

    def arrived(side, k, c):
        ref = buf.at[side, k, piece(c)]
        pltpu.make_async_copy(ref, ref, recv_sem.at[side, k, c]).wait()

    for c in range(chunks):
        for side in range(2):
            local(side, c).start()
    places[0] = jnp.broadcast_to(positives[...], places.shape[1:])

    barrier = pltpu.get_barrier_semaphore()
    for offset in (-3, -2, -1, 1, 2, 3):
        pl.semaphore_signal(barrier, inc=1, device_id=(at(offset),), device_id_type=MESH)
    pl.semaphore_wait(barrier, 6)

    def send_near(c):
        near_text(c).start()
        near_image(c).start()

    def send_far(c):
        @pl.when((place != 3))
        def _():
            far_text(c).start()

        @pl.when((place != 0))
        def _():
            far_image(c).start()

    for c in range(chunks):
        send_near(c)
    for c in range(chunks):
        send_far(c)
    for k in range(1, 4):
        place_copy(k).start()

    for c in range(chunks):
        for side in range(2):
            local(side, c).wait()
    for side in range(2):
        a_high, a_low = split(buf[1 - side, 0])
        three[side] = jnp.concatenate([a_high, a_high, a_low], axis=1)

    def scored(side, parts):
        b_high, b_low = split(jnp.concatenate([buf[side, k, pl.ds(row, size), :] for k, row, size in parts], axis=0))
        return b_high, b_low, dot(three[side], jnp.concatenate([b_high, b_low, b_high], axis=1), 1)

    def finished(side, parts, b_high, b_low, scores, first):
        out = (grad_image, grad_text)[side]
        logits = 10.0 * scores - 10.0
        columns = []
        for k, row, size in parts:
            wanted = places[0 if side == 0 else k, 0:1, pl.ds(row, size)]
            block = lax.rem(me - k + n, n) if side == 0 else me
            lanes = lax.broadcasted_iota(jnp.int32, (1, size), 1) + row
            columns.append(jnp.where(wanted == block * rows + lanes, lanes, -1))
        column = jnp.concatenate(columns, axis=1)
        match = lax.broadcasted_iota(jnp.int32, scores.shape, 0) == column
        decay = jnp.exp(-jnp.abs(logits))
        inverse = 1.0 / (1.0 + decay)
        sigmoid = jnp.where(logits >= 0.0, inverse, decay * inverse)
        weight = (sigmoid - match.astype(F32)) * (10.0 / rows)
        w_high, w_low = split(weight)
        grad = dot(jnp.concatenate([w_high, w_low, w_high], axis=1),
                   jnp.concatenate([b_high, b_high, b_low], axis=0), 0)
        if first:
            out[...] = grad
        else:
            out[...] += grad
        if side == 0:
            signed = jnp.where(match, -logits, logits)
            part = jnp.maximum(signed, 0.0) + jnp.log1p(decay)
            folded = part[:, :128]
            for s in range(128, part.shape[1], 128):
                folded += part[:, s:s + 128]
            if first:
                total[...] = folded
            else:
                total[...] += folded

    def units(text_parts, image_parts, first=False):
        a = scored(0, text_parts)
        b = scored(1, image_parts)
        finished(0, text_parts, *a, first)
        finished(1, image_parts, *b, first)

    units([(0, 0, rows)], [(0, 0, rows)], first=True)
    for k in range(1, 4):
        place_copy(k).wait_recv()

    early_text, early_image = 3 - 2 * odd, 1 + 2 * odd
    late_text, late_image = 1 + 2 * odd, 3 - 2 * odd

    def near_step(c):
        arrived(0, early_text, c)
        arrived(1, early_image, c)

        @pl.when((place == 2))
        def _():
            relay_text(c).start()

        @pl.when((place == 1))
        def _():
            relay_image(c).start()

    def step(c, carry):
        arrived(0, 2, c)
        pass_text(c).start()
        arrived(1, 2, c)
        pass_image(c).start()

        @pl.when(c + 1 < chunks)
        def _():
            near_step(c + 1)

        arrived(0, late_text, c)
        arrived(1, late_image, c)
        row = pl.multiple_of(c * chunk, chunk)
        units([(2, row, chunk), (late_text, row, chunk)], [(2, row, chunk), (late_image, row, chunk)])

        @pl.when((c == chunks // 2 - 1) | (c == chunks - 2))
        def _():
            row = pl.multiple_of((c // (chunks // 2)) * (rows // 2), rows // 2)
            units([(early_text, row, rows // 2)], [(early_image, row, rows // 2)])

        return carry

    near_step(0)
    lax.fori_loop(0, chunks, step, 0)
    loss[...] = jnp.sum(total[...].T, axis=0, keepdims=True) * (1.0 / rows)

    for c in range(chunks):
        near_text(c).wait_send()
        near_image(c).wait_send()
        pass_text(c).wait_send()
        pass_image(c).wait_send()

        @pl.when((place != 3))
        def _():
            far_text(c).wait_send()

        @pl.when((place != 0))
        def _():
            far_image(c).wait_send()

        @pl.when((place == 2))
        def _():
            relay_text(c).wait_send()

        @pl.when((place == 1))
        def _():
            relay_image(c).wait_send()
    for k in range(1, 4):
        place_copy(k).wait_send()


def per_device(n, image_embed, text_embed, positives):
    rows, width = image_embed.shape
    chunk = CHUNK if rows % (4 * CHUNK) == 0 else rows // 4
    chunks = rows // chunk
    vmem = pl.BlockSpec(memory_space=pltpu.VMEM)
    anywhere = pl.BlockSpec(memory_space=pl.ANY)
    block = jax.ShapeDtypeStruct((rows, width), F32)
    grad_image, grad_text, loss = pl.pallas_call(
        functools.partial(kernel, n, chunk),
        out_shape=(block, block, jax.ShapeDtypeStruct((1, rows), F32)),
        in_specs=[anywhere, anywhere, vmem],
        out_specs=(vmem, vmem, vmem),
        scratch_shapes=[
            pltpu.VMEM((2, 4, rows, width), F32),
            pltpu.VMEM((2, rows, 3 * width), BF16),
            pltpu.VMEM((rows, 128), F32),
            pltpu.VMEM((4, 8, rows), jnp.int32),
            pltpu.SemaphoreType.DMA((7, chunks)),
            pltpu.SemaphoreType.DMA((2, 4, chunks)),
            pltpu.SemaphoreType.DMA((4,)),
            pltpu.SemaphoreType.DMA((4,)),
        ],
        compiler_params=pltpu.CompilerParams(
            collective_id=0, has_side_effects=True, vmem_limit_bytes=60 * 2**20),
        cost_estimate=pl.CostEstimate(
            flops=2 * 16 * 3 * rows * rows * width, bytes_accessed=16 * rows * width,
            transcendentals=8 * rows * rows),
    )(image_embed, text_embed, positives.reshape(1, rows))
    return loss.reshape(rows), grad_image, grad_text


def solution(mesh):
    placed = (P("dp", None), P("dp", None), P("dp"))
    return jax.shard_map(
        functools.partial(per_device, mesh.shape["dp"]),
        mesh=mesh,
        in_specs=placed,
        out_specs=(P("dp"), P("dp", None), P("dp", None)),
        check_vma=False,
    )
```

```python
import functools

import jax
import jax.numpy as jnp
from jax import lax
from jax.experimental import pallas as pl
from jax.experimental.pallas import tpu as pltpu
from jax.sharding import PartitionSpec as P

MESH = pl.DeviceIdType.MESH
F32 = jnp.float32
BF16 = jnp.bfloat16
CHUNK = 128


def split(x):
    high = x.astype(BF16)
    return high, (x - high.astype(F32)).astype(BF16)


def dot(a, b, contract):
    return lax.dot_general(a, b, (((1,), (contract,)), ((), ())), preferred_element_type=F32)


def kernel(n, chunk, image, text, positives, grad_image, grad_text, loss, buf, three, total, places,
           send_sem, recv_sem, place_send, place_recv):
    rows = image.shape[0]
    chunks = rows // chunk
    me = lax.axis_index("dp")
    odd = lax.rem(me, 2)
    place = lax.rem(me, 4)
    partner = me + 1 - 2 * odd

    def at(offset):
        return lax.rem(me + offset + n, n)

    def piece(c):
        return pl.ds(pl.multiple_of(c * chunk, chunk), chunk)

    def remote(src, side, slot, c, lane, device):
        return pltpu.make_async_remote_copy(
            src_ref=src, dst_ref=buf.at[side, slot, piece(c)],
            send_sem=send_sem.at[lane, c], recv_sem=recv_sem.at[side, slot, c],
            device_id=(device,), device_id_type=MESH)

    def far_text(c):
        return remote(text.at[piece(c)], 0, 2, c, 0, at(2))

    def far_image(c):
        return remote(image.at[piece(c)], 1, 2, c, 1, at(-2))

    def relay_text(c):
        return remote(buf.at[0, 3, piece(c)], 0, 2, c, 6, at(-1))

    def relay_image(c):
        return remote(buf.at[1, 3, piece(c)], 1, 2, c, 6, at(1))

    def near_text(c):
        return remote(text.at[piece(c)], 0, 2 * odd + 1, c, 2, at(1 + 2 * odd))

    def near_image(c):
        return remote(image.at[piece(c)], 1, 3 - 2 * odd, c, 3, at(2 * odd - 3))

    def pass_text(c):
        return remote(buf.at[0, 2, piece(c)], 0, 3 - 2 * odd, c, 4, partner)

    def pass_image(c):
        return remote(buf.at[1, 2, piece(c)], 1, 2 * odd + 1, c, 5, partner)

    def local(side, c):
        src = (text, image)[side]
        return pltpu.make_async_copy(src.at[piece(c)], buf.at[side, 0, piece(c)], recv_sem.at[side, 0, c])

    def place_copy(k):
        return pltpu.make_async_remote_copy(
            src_ref=places.at[0], dst_ref=places.at[k], send_sem=place_send.at[k],
            recv_sem=place_recv.at[k], device_id=(at(-k),), device_id_type=MESH)

    def arrived(side, k, c):
        ref = buf.at[side, k, piece(c)]
        pltpu.make_async_copy(ref, ref, recv_sem.at[side, k, c]).wait()

    for c in range(chunks):
        for side in range(2):
            local(side, c).start()
    places[0] = jnp.broadcast_to(positives[...], places.shape[1:])

    barrier = pltpu.get_barrier_semaphore()
    for offset in (-3, -2, -1, 1, 2, 3):
        pl.semaphore_signal(barrier, inc=1, device_id=(at(offset),), device_id_type=MESH)
    pl.semaphore_wait(barrier, 6)

    def send_near(c):
        near_text(c).start()
        near_image(c).start()

    def send_far(c):
        @pl.when((place != 3))
        def _():
            far_text(c).start()

        @pl.when((place != 0))
        def _():
            far_image(c).start()

    for c in range(chunks):
        send_near(c)
    for c in range(chunks):
        send_far(c)
    for k in range(1, 4):
        place_copy(k).start()

    for c in range(chunks):
        for side in range(2):
            local(side, c).wait()
    for side in range(2):
        a_high, a_low = split(buf[1 - side, 0])
        three[side] = jnp.concatenate([a_high, a_high, a_low], axis=1)

    def scored(side, parts):
        b_high, b_low = split(jnp.concatenate([buf[side, k, pl.ds(row, size), :] for k, row, size in parts], axis=0))
        return b_high, b_low, dot(three[side], jnp.concatenate([b_high, b_low, b_high], axis=1), 1)

    def finished(side, parts, b_high, b_low, scores, first):
        out = (grad_image, grad_text)[side]
        logits = 10.0 * scores - 10.0
        columns = []
        for k, row, size in parts:
            wanted = places[0 if side == 0 else k, 0:1, pl.ds(row, size)]
            block = lax.rem(me - k + n, n) if side == 0 else me
            lanes = lax.broadcasted_iota(jnp.int32, (1, size), 1) + row
            columns.append(jnp.where(wanted == block * rows + lanes, lanes, -1))
        column = jnp.concatenate(columns, axis=1)
        match = lax.broadcasted_iota(jnp.int32, scores.shape, 0) == column
        decay = jnp.exp(-jnp.abs(logits))
        inverse = 1.0 / (1.0 + decay)
        sigmoid = jnp.where(logits >= 0.0, inverse, decay * inverse)
        weight = (sigmoid - match.astype(F32)) * (10.0 / rows)
        w_high, w_low = split(weight)
        grad = dot(jnp.concatenate([w_high, w_low, w_high], axis=1),
                   jnp.concatenate([b_high, b_high, b_low], axis=0), 0)
        if first:
            out[...] = grad
        else:
            out[...] += grad
        if side == 0:
            signed = jnp.where(match, -logits, logits)
            part = jnp.maximum(signed, 0.0) + jnp.log1p(decay)
            folded = part[:, :128]
            for s in range(128, part.shape[1], 128):
                folded += part[:, s:s + 128]
            if first:
                total[...] = folded
            else:
                total[...] += folded

    def units(text_parts, image_parts, first=False):
        a = scored(0, text_parts)
        b = scored(1, image_parts)
        finished(0, text_parts, *a, first)
        finished(1, image_parts, *b, first)

    units([(0, 0, rows)], [(0, 0, rows)], first=True)
    for k in range(1, 4):
        place_copy(k).wait_recv()

    early_text, early_image = 3 - 2 * odd, 1 + 2 * odd
    late_text, late_image = 1 + 2 * odd, 3 - 2 * odd

    def near_step(c):
        arrived(0, early_text, c)
        arrived(1, early_image, c)

        @pl.when((place == 2))
        def _():
            relay_text(c).start()

        @pl.when((place == 1))
        def _():
            relay_image(c).start()

    def step(c, carry):
        arrived(0, 2, c)
        pass_text(c).start()
        arrived(1, 2, c)
        pass_image(c).start()

        @pl.when(c + 2 < chunks)
        def _():
            near_step(c + 2)

        arrived(0, late_text, c)
        arrived(1, late_image, c)
        row = pl.multiple_of(c * chunk, chunk)
        units([(2, row, chunk), (late_text, row, chunk)], [(2, row, chunk), (late_image, row, chunk)])

        @pl.when((c == chunks // 2 - 2) | (c == chunks - 3))
        def _():
            row = pl.multiple_of((c // (chunks - 3)) * (rows // 2), rows // 2)
            units([(early_text, row, rows // 2)], [(early_image, row, rows // 2)])

        return carry

    near_step(0)
    near_step(1)
    lax.fori_loop(0, chunks, step, 0)
    loss[...] = jnp.sum(total[...].T, axis=0, keepdims=True) * (1.0 / rows)

    for c in range(chunks):
        near_text(c).wait_send()
        near_image(c).wait_send()
        pass_text(c).wait_send()
        pass_image(c).wait_send()

        @pl.when((place != 3))
        def _():
            far_text(c).wait_send()

        @pl.when((place != 0))
        def _():
            far_image(c).wait_send()

        @pl.when((place == 2))
        def _():
            relay_text(c).wait_send()

        @pl.when((place == 1))
        def _():
            relay_image(c).wait_send()
    for k in range(1, 4):
        place_copy(k).wait_send()


def per_device(n, image_embed, text_embed, positives):
    rows, width = image_embed.shape
    chunk = CHUNK if rows % (4 * CHUNK) == 0 else rows // 4
    chunks = rows // chunk
    vmem = pl.BlockSpec(memory_space=pltpu.VMEM)
    anywhere = pl.BlockSpec(memory_space=pl.ANY)
    block = jax.ShapeDtypeStruct((rows, width), F32)
    grad_image, grad_text, loss = pl.pallas_call(
        functools.partial(kernel, n, chunk),
        out_shape=(block, block, jax.ShapeDtypeStruct((1, rows), F32)),
        in_specs=[anywhere, anywhere, vmem],
        out_specs=(vmem, vmem, vmem),
        scratch_shapes=[
            pltpu.VMEM((2, 4, rows, width), F32),
            pltpu.VMEM((2, rows, 3 * width), BF16),
            pltpu.VMEM((rows, 128), F32),
            pltpu.VMEM((4, 8, rows), jnp.int32),
            pltpu.SemaphoreType.DMA((7, chunks)),
            pltpu.SemaphoreType.DMA((2, 4, chunks)),
            pltpu.SemaphoreType.DMA((4,)),
            pltpu.SemaphoreType.DMA((4,)),
        ],
        compiler_params=pltpu.CompilerParams(
            collective_id=0, has_side_effects=True, vmem_limit_bytes=60 * 2**20),
        cost_estimate=pl.CostEstimate(
            flops=2 * 16 * 3 * rows * rows * width, bytes_accessed=16 * rows * width,
            transcendentals=8 * rows * rows),
    )(image_embed, text_embed, positives.reshape(1, rows))
    return loss.reshape(rows), grad_image, grad_text


def solution(mesh):
    placed = (P("dp", None), P("dp", None), P("dp"))
    return jax.shard_map(
        functools.partial(per_device, mesh.shape["dp"]),
        mesh=mesh,
        in_specs=placed,
        out_specs=(P("dp"), P("dp", None), P("dp", None)),
        check_vma=False,
    )
```
